32 devices in a mesh: groups: 2 (over x), owners: 16 (over z, y, core).
Axes of the slice: x: 2, y: 2, z: 4, core: 2. Of those that a mesh axis runs over, the one named last changes fastest.
Arguments:
- embeddings: float32 [24576, 768], P(('groups', 'owners')), parts along dimension 0, may hold values from -1100 to 1100
- cluster_of: int32 [24576], P(('groups', 'owners')), parts along dimension 0, may hold values from 0 to 7, as said below
Outputs:
- best_score: float32 [24576], P(('groups', 'owners')), parts along dimension 0
The draws below stay inside these ranges and needn't reach their ends.
There are 2 independent parts, one for each index of `groups`. The reference program is written for one: setup_inputs(seed, part) draws one part's arguments, and reference() takes and returns one part's arrays. A program takes and returns all parts, laid end to end along the dimension named above; each array names one. Nothing has to cross between parts.
Inputs may be any that keep to these rules, and one draw needn't show every extreme that they name: `cluster_of`: the rows of one ingest device (aligned blocks of 768 rows) hold at most 128 rows of any one cluster; in every draw some cluster has exactly 128 rows on every ingest device.
All inputs are finite; a program needn't handle non-finite values.
Results may differ from the reference program's by a relative error of at most 0.00043.
Values may be sent and summed in bfloat16 or wider, within the bound.
No kernel may reach another device: no remote copies, remote signals or barrier semaphores. Data moves between devices by JAX's collectives and lax.ppermute only.
A program may use at most 64 MiB of HBM per device.

```python
import jax
import jax.numpy as jnp
from jax import lax

D = 768
SLOTS = 1024
CAP = 64
CLUSTERS = 8
ROWS_DEV = 768
ROWS = 12288
N_OWNERS = 16


def layout(key):
    span_slots = 2 * CAP
    popular = jax.random.randint(jax.random.fold_in(key, 11), (CLUSTERS,), 0, 4)
    forced = jax.random.randint(jax.random.fold_in(key, 12), (), 0, CLUSTERS)
    cluster_bias = popular * 2048 + jnp.where(jnp.arange(CLUSTERS) == forced, 65536, 0)
    noise_term = jax.random.randint(jax.random.fold_in(key, 13), (N_OWNERS, CLUSTERS, span_slots), 0, 4096)
    tiebreak = jnp.arange(CLUSTERS * span_slots, dtype=jnp.int32).reshape(CLUSTERS, span_slots)
    slot_score = (noise_term + cluster_bias[None, :, None]) * (CLUSTERS * span_slots) + tiebreak[None, :, :]
    flat_score = slot_score.reshape(N_OWNERS, CLUSTERS * span_slots).astype(jnp.int32)
    chosen = lax.top_k(flat_score, ROWS_DEV)[1].astype(jnp.int32)
    chosen_cluster = chosen // span_slots
    chosen_rank = chosen % span_slots
    shuffle_keys = jax.random.split(jax.random.fold_in(key, 14), N_OWNERS)
    shuffle = jax.vmap(lambda single: jax.random.permutation(single, ROWS_DEV))(shuffle_keys).astype(jnp.int32)
    device_index = jnp.arange(N_OWNERS, dtype=jnp.int32)[:, None]
    cluster_rows = jnp.zeros((N_OWNERS, ROWS_DEV), jnp.int32).at[device_index, shuffle].set(chosen_cluster)
    rank_rows = jnp.zeros((N_OWNERS, ROWS_DEV), jnp.int32).at[device_index, shuffle].set(chosen_rank)
    pairing = jax.random.permutation(jax.random.fold_in(key, 15), N_OWNERS).astype(jnp.int32)
    pair_of = jnp.zeros((N_OWNERS,), jnp.int32).at[pairing].set(jnp.arange(N_OWNERS, dtype=jnp.int32) // 2)
    return (cluster_rows.reshape(ROWS), rank_rows.reshape(ROWS), pair_of)


def draw_cluster_of(key, part):
    cluster_rows, rank_rows, pair_of = layout(key)
    return cluster_rows


def draw_embeddings(key, part):
    cluster_rows, rank_rows, pair_of = layout(key)
    key = jax.random.fold_in(key, 3)
    source = jnp.arange(ROWS, dtype=jnp.int32) // ROWS_DEV
    document = (cluster_rows * (N_OWNERS // 2) + pair_of[source]) * (2 * CAP) + rank_rows
    doc_key = jax.random.fold_in(key, 21)
    strength_key = jax.random.fold_in(key, 22)
    doc_vector = jax.vmap(lambda doc_index: jax.random.truncated_normal(jax.random.fold_in(doc_key, doc_index), -4.0, 4.0, (D,)))(document)
    strength = jax.vmap(lambda doc_index: jax.random.uniform(jax.random.fold_in(strength_key, doc_index), (), jnp.float32, 0.3, 5.0))(document)
    column_scale = jnp.exp(jax.random.uniform(jax.random.fold_in(key, 24), (D,), jnp.float32, jnp.log(0.4), jnp.log(4.0)))
    noise_term = jax.random.truncated_normal(jax.random.fold_in(key, 23), -4.0, 4.0, (ROWS, D))
    row_scale = jnp.exp(jax.random.uniform(jax.random.fold_in(key, 26), (ROWS, 1), jnp.float32, jnp.log(0.3), jnp.log(3.0)))
    base_rows = strength[:, None] * doc_vector + noise_term
    return (row_scale * column_scale[None, :] * base_rows).astype(jnp.float32)


def setup_inputs(seed: int = 0, part: int = 0) -> dict:
    arg_keys = jax.random.split(jax.random.key(seed), 3)
    own_keys = jax.random.split(jax.random.fold_in(arg_keys[2], part), 3)
    embeddings = draw_embeddings(jax.random.fold_in(jax.random.fold_in(arg_keys[2], part), 71), part)
    cluster_of = draw_cluster_of(jax.random.fold_in(jax.random.fold_in(arg_keys[2], part), 71), part)
    return dict(embeddings=embeddings, cluster_of=cluster_of)


def reference(embeddings, cluster_of):
    scale = lax.rsqrt(lax.optimization_barrier(jnp.sum(embeddings * embeddings, axis=1, keepdims=True)) + 1e-06)
    unit_rows = (embeddings * scale).astype(jnp.bfloat16)
    sort_order = jnp.argsort(cluster_of, stable=True).astype(jnp.int32)
    sorted_ids = cluster_of[sort_order]
    sorted_units = unit_rows[sort_order].astype(jnp.float32)
    window = 2 * SLOTS
    counts = jax.ops.segment_sum(jnp.ones((ROWS,), jnp.int32), cluster_of, CLUSTERS)
    offsets = (jnp.cumsum(counts) - counts).astype(jnp.int32)
    padded_units = jnp.concatenate([sorted_units, jnp.zeros((window, D), jnp.float32)], axis=0)
    padded_ids = jnp.concatenate([sorted_ids, jnp.full((window,), -1, jnp.int32)], axis=0)
    diagonal = jnp.arange(window, dtype=jnp.int32)

    def cluster_best(which):
        first_row = offsets[which]
        window_rows = lax.dynamic_slice_in_dim(padded_units, first_row, window, 0)
        window_ids = lax.dynamic_slice_in_dim(padded_ids, first_row, window, 0)
        member = window_ids == which
        scores = jnp.dot(window_rows, window_rows.T, precision=lax.Precision.HIGHEST, preferred_element_type=jnp.float32)
        keep_mask = member[None, :] & (diagonal[:, None] != diagonal[None, :])
        scores = jnp.where(keep_mask, scores, -4.0)
        return lax.optimization_barrier(jnp.max(scores, axis=1))
    window_best = lax.map(cluster_best, jnp.arange(CLUSTERS, dtype=jnp.int32))
    within = jnp.arange(ROWS, dtype=jnp.int32) - offsets[sorted_ids]
    sorted_best = window_best[sorted_ids, within]
    best_score = jnp.zeros((ROWS,), jnp.float32).at[sort_order].set(sorted_best)
    return jnp.maximum(best_score, -1.0)
```

```python
import functools

import jax
import jax.numpy as jnp
from jax import lax
from jax.experimental import pallas as pl
from jax.experimental.pallas import tpu as pltpu
from jax.sharding import PartitionSpec as P

SLOTS = 1024
FLOOR = -4.0
DEAD = 4.0
VMEM_LIMIT = 40 * 2**20
LANES = 128


def block_mask(shape, lower, step):
    return lax.broadcasted_iota(jnp.int32, shape, 0) * step + lower


def row_slots(relative, clusters, capacity):
    rows = relative.shape[1]
    ids = lax.broadcasted_iota(jnp.int32, (clusters, LANES), 0)
    earlier = (
        lax.broadcasted_iota(jnp.int32, (LANES, LANES), 0)
        < lax.broadcasted_iota(jnp.int32, (LANES, LANES), 1)
    ).astype(jnp.bfloat16)
    carry = jnp.zeros((clusters, 1), jnp.float32)
    places = []
    for first in range(0, rows, LANES):
        part = relative[:, first : first + LANES]
        member = (ids == part).astype(jnp.float32)
        before = carry + jnp.dot(
            member.astype(jnp.bfloat16), earlier, preferred_element_type=jnp.float32
        )
        place = jnp.sum(before * member, axis=0, keepdims=True)
        places.append(part * capacity + place.astype(jnp.int32))
        carry = carry + jnp.sum(member, axis=1, keepdims=True)
    return jnp.concatenate(places, axis=1), carry


def pack_kernel(first_block, steps, clusters, capacity, relative_ref, rows_ref, *refs):
    *block_refs, slot_ref, unit_ref, pick_ref, count_ref = refs
    step = pl.program_id(0)
    tile = rows_ref.shape[0]
    values = rows_ref[...]
    scale = lax.rsqrt(jnp.sum(values * values, axis=1, keepdims=True) + 1e-06)
    unit_ref[pl.ds(pl.multiple_of(step * tile, tile), tile), :] = (values * scale).astype(jnp.bfloat16)

    @pl.when(step == 0)
    def _():
        slots, counts = row_slots(relative_ref[...], clusters, capacity)
        slot_ref[...] = slots
        count_ref[...] = jnp.broadcast_to(counts, count_ref.shape)
        wanted = lax.broadcasted_iota(jnp.int32, pick_ref.shape, 0) + first_block * capacity
        pick_ref[...] = (wanted == slots).astype(jnp.float32).astype(jnp.bfloat16)

    @pl.when(step == steps - 1)
    def _():
        lane = lax.broadcasted_iota(jnp.int32, (1, LANES), 1)
        done = 0
        for block_ref in block_refs:
            for start in range(0, block_ref.shape[0], capacity):
                size = capacity
                block = jnp.dot(
                    pick_ref[done : done + size, :], unit_ref[...], preferred_element_type=jnp.float32
                )
                which = first_block + done // capacity
                count = count_ref[which : which + 1, :]
                place = lax.broadcasted_iota(jnp.int32, (size, LANES), 0).astype(jnp.float32)
                mark = jnp.where((place >= count) & (lane == 0), DEAD, 0.0)
                block_ref[start : start + size, :LANES] = (block[:, :LANES] + mark).astype(jnp.bfloat16)
                block_ref[start : start + size, LANES:] = block[:, LANES:].astype(jnp.bfloat16)
                done += size


def pack(relative, embeddings, first_block, block_counts, clusters, capacity):
    rows, width = embeddings.shape
    steps = 3 if rows % 384 == 0 else 1
    total = sum(block_counts) * capacity
    whole = lambda shape: pl.BlockSpec(shape, lambda step: (0, 0))
    shapes = [(count * capacity, width) for count in block_counts]
    *blocks, slots = pl.pallas_call(
        functools.partial(pack_kernel, first_block, steps, clusters, capacity),
        grid=(steps,),
        in_specs=[whole((1, rows)), pl.BlockSpec((rows // steps, width), lambda step: (step, 0))],
        out_specs=[whole(shape) for shape in shapes] + [whole((1, rows))],
        out_shape=[jax.ShapeDtypeStruct(shape, jnp.bfloat16) for shape in shapes]
        + [jax.ShapeDtypeStruct((1, rows), jnp.int32)],
        scratch_shapes=[
            pltpu.VMEM((rows, width), jnp.bfloat16),
            pltpu.VMEM((total, rows), jnp.bfloat16),
            pltpu.VMEM((clusters, LANES), jnp.float32),
        ],
        compiler_params=pltpu.CompilerParams(vmem_limit_bytes=VMEM_LIMIT),
        cost_estimate=pl.CostEstimate(
            flops=2 * total * rows * width, bytes_accessed=rows * width * 4 + total * width * 2, transcendentals=rows
        ),
    )(relative, embeddings)
    return blocks, slots


def pieces(refs, tile):
    groups, current, held = [], [], 0
    for ref in refs:
        start = 0
        while start < ref.shape[0]:
            size = min(tile - held, ref.shape[0] - start)
            current.append((ref, start, size))
            start += size
            held += size
            if held == tile:
                groups.append(current)
                current, held = [], 0
    if current:
        groups.append(current)
    return groups


def load(group):
    parts = [ref[start : start + size, :] for ref, start, size in group]
    return parts[0] if len(parts) == 1 else jnp.concatenate(parts, axis=0)


def score_kernel(n_queries, n_keys, has_start, self_offset, *refs):
    query_refs = refs[:n_queries]
    key_refs = refs[n_queries : n_queries + n_keys]
    start_ref = refs[n_queries + n_keys] if has_start else None
    best_ref = refs[-1]
    key_groups = pieces(key_refs, 512)
    keys_and_bias = []
    query_first = 0
    for query_group in pieces(query_refs, 256):
        query = load(query_group)
        wide = query.shape[0]
        best = jnp.full((8, wide), FLOOR, jnp.float32)
        key_first = 0
        for key_group in key_groups:
            key = load(key_group)
            deep = key.shape[0]
            scores = lax.dot_general(key, query, (((1,), (1,)), ((), ())), preferred_element_type=jnp.float32)
            dead = key[:, :1].astype(jnp.float32) > 2.0
            drop = jnp.where(dead, 2 * FLOOR, 0.0)
            scores = scores + drop
            if self_offset is not None:
                shift = query_first + self_offset - key_first
                if -wide < shift < deep:
                    own = lax.broadcasted_iota(jnp.int32, scores.shape, 0) == (
                        lax.broadcasted_iota(jnp.int32, scores.shape, 1) + shift
                    )
                    scores = jnp.where(own, FLOOR, scores)
            best = jnp.maximum(best, jnp.max(scores.reshape(deep // 8, 8, wide), axis=0))
            key_first += deep
        row = jnp.max(best, axis=0, keepdims=True)
        for lane in range(0, wide, LANES):
            at = (query_first + lane) // LANES
            part = row[:, lane : lane + LANES]
            if start_ref is not None:
                part = jnp.maximum(part, start_ref[at : at + 1, :])
            best_ref[at : at + 1, :] = part
        query_first += wide


def score(queries, keys, self_offset, start=None):
    n_query = sum(block.shape[0] for block in queries)
    n_key = sum(block.shape[0] for block in keys)
    width = queries[0].shape[1]
    args = [*queries, *keys] + ([] if start is None else [start])
    return pl.pallas_call(
        functools.partial(score_kernel, len(queries), len(keys), start is not None, self_offset),
        in_specs=[pl.BlockSpec(memory_space=pltpu.VMEM)] * len(args),
        out_specs=pl.BlockSpec(memory_space=pltpu.VMEM),
        out_shape=jax.ShapeDtypeStruct((n_query // LANES, LANES), jnp.float32),
        compiler_params=pltpu.CompilerParams(vmem_limit_bytes=VMEM_LIMIT),
        cost_estimate=pl.CostEstimate(
            flops=2 * n_query * n_key * width, bytes_accessed=(n_query + n_key) * width * 2, transcendentals=0
        ),
    )(*args)


def lookup_kernel(capacity, slot_ref, answer_ref, out_ref):
    slots = slot_ref[...]
    clusters = answer_ref.shape[0]
    shift = capacity.bit_length() - 1
    place = lax.bitwise_and(slots, capacity - 1)
    which = lax.shift_right_logical(slots, shift)
    rows = slots.shape[1]
    pick = (lax.broadcasted_iota(jnp.int32, (capacity, rows), 0) == place).astype(jnp.float32).astype(jnp.bfloat16)
    rest = answer_ref[...]
    total = jnp.zeros((clusters, rows), jnp.float32)
    for _ in range(3):
        part = rest.astype(jnp.bfloat16)
        rest = rest - part.astype(jnp.float32)
        total = total + jnp.dot(part, pick, preferred_element_type=jnp.float32)
    mine = lax.broadcasted_iota(jnp.int32, (clusters, rows), 0) == which
    found = jnp.sum(jnp.where(mine, total, 0.0), axis=0, keepdims=True)
    out_ref[...] = jnp.maximum(found, -1.0)


def lookup(slots, answers, capacity):
    return pl.pallas_call(
        functools.partial(lookup_kernel, capacity),
        in_specs=[pl.BlockSpec(memory_space=pltpu.VMEM)] * 2,
        out_specs=pl.BlockSpec(memory_space=pltpu.VMEM),
        out_shape=jax.ShapeDtypeStruct(slots.shape, jnp.float32),
        compiler_params=pltpu.CompilerParams(vmem_limit_bytes=VMEM_LIMIT),
    )(slots, answers)


def by_xor(value, axis, mask):
    return lax.ppermute(value, axis, [(source, source ^ mask) for source in range(lax.axis_size(axis))])


def on_device(embeddings, cluster_of):
    owners = lax.axis_size("owners")
    clusters = owners // 2
    capacity = SLOTS // clusters
    rows = embeddings.shape[0]
    cluster_row = cluster_of.reshape(1, rows)
    chip = lax.axis_index("owners") // 2
    same_core = [list(range(core, owners, 2)) for core in range(2)]
    if clusters == 8:
        relative = cluster_row ^ chip
        far_out, slots = pack(relative, embeddings, 4, [1, 1, 1, 1], clusters, capacity)
        far = [by_xor(block, "owners", 2 * mask) for block, mask in zip(far_out, (4, 5, 6, 7))]
        near_out, _ = pack(relative, embeddings, 0, [1, 1, 1, 1], clusters, capacity)
        near = [near_out[0]] + [by_xor(block, "owners", 2 * mask) for block, mask in zip(near_out[1:], (1, 2, 3))]
        near_other = [by_xor(block, "owners", 1) for block in near]
        near_best = score(near, near + near_other, 0)
        far_other = [by_xor(block, "owners", 1) for block in far]
        near_best = score(near, far + far_other, None, near_best)
        far_best = score(far, far + near + near_other + far_other, 0)
        best = jnp.concatenate([near_best, far_best], axis=0)
        order = jnp.arange(clusters, dtype=jnp.int32) ^ chip
        best = jnp.take(best, order, axis=0)
        answers = lax.all_to_all(best, "owners", 0, 0, axis_index_groups=same_core, tiled=True)
        answers = jnp.take(answers, order, axis=0)
    else:
        (outgoing,), slots = pack(cluster_row, embeddings, 0, [clusters], clusters, capacity)
        own = lax.all_to_all(
            outgoing.reshape(clusters, capacity, -1), "owners", 0, 0, axis_index_groups=same_core, tiled=True
        ).reshape(SLOTS, -1)
        best = score([own], [own, by_xor(own, "owners", 1)], 0).reshape(clusters, capacity)
        answers = lax.all_to_all(best, "owners", 0, 0, axis_index_groups=same_core, tiled=True)
    return lookup(slots, answers, capacity).reshape(rows)


def solution(mesh):
    placed = (P(("groups", "owners"), None), P(("groups", "owners")))
    return jax.shard_map(
        on_device, mesh=mesh, in_specs=placed, out_specs=P(("groups", "owners")), check_vma=False
    )
```

```python
import functools

import jax
import jax.numpy as jnp
from jax import lax
from jax.experimental import pallas as pl
from jax.experimental.pallas import tpu as pltpu
from jax.sharding import PartitionSpec as P

SLOTS = 1024
FLOOR = -4.0
DEAD = 4.0
VMEM_LIMIT = 40 * 2**20
LANES = 128


def row_slots(relative, clusters, capacity):
    rows = relative.shape[1]
    ids = lax.broadcasted_iota(jnp.int32, (clusters, LANES), 0)
    earlier = (
        lax.broadcasted_iota(jnp.int32, (LANES, LANES), 0)
        < lax.broadcasted_iota(jnp.int32, (LANES, LANES), 1)
    ).astype(jnp.bfloat16)
    carry = jnp.zeros((clusters, 1), jnp.float32)
    places = []
    for first in range(0, rows, LANES):
        part = relative[:, first : first + LANES]
        member = (ids == part).astype(jnp.float32)
        before = carry + jnp.dot(
            member.astype(jnp.bfloat16), earlier, preferred_element_type=jnp.float32
        )
        place = jnp.sum(before * member, axis=0, keepdims=True)
        places.append(part * capacity + place.astype(jnp.int32))
        carry = carry + jnp.sum(member, axis=1, keepdims=True)
    return jnp.concatenate(places, axis=1), carry


def pack_kernel(first_block, mixed, clusters, capacity, cluster_ref, rows_ref, *refs):
    *block_refs, slot_ref, held_ref, unit_ref, pick_ref, sems = refs
    steps, tile, _ = held_ref.shape
    copies = [
        pltpu.make_async_copy(rows_ref.at[pl.ds(step * tile, tile), :], held_ref.at[step], sems.at[step])
        for step in range(steps)
    ]
    for copy in copies:
        copy.start()
    relative = cluster_ref[...]
    if mixed:
        relative = lax.bitwise_xor(relative, lax.axis_index("owners") // 2)
    slots, counts = row_slots(relative, clusters, capacity)
    slot_ref[...] = slots
    wanted = lax.broadcasted_iota(jnp.int32, pick_ref.shape, 0) + first_block * capacity
    pick_ref[...] = (wanted == slots).astype(jnp.float32).astype(jnp.bfloat16)
    for step, copy in enumerate(copies):
        copy.wait()
        values = held_ref[step]
        scale = lax.rsqrt(jnp.sum(values * values, axis=1, keepdims=True) + 1e-06)
        unit_ref[step * tile : (step + 1) * tile, :] = (values * scale).astype(jnp.bfloat16)
    lane = lax.broadcasted_iota(jnp.int32, (capacity, LANES), 1)
    place = lax.broadcasted_iota(jnp.int32, (capacity, LANES), 0).astype(jnp.float32)
    done = 0
    for block_ref in block_refs:
        for start in range(0, block_ref.shape[0], capacity):
            block = jnp.dot(
                pick_ref[done : done + capacity, :], unit_ref[...], preferred_element_type=jnp.float32
            )
            which = first_block + done // capacity
            mark = jnp.where((place >= counts[which : which + 1, :]) & (lane == 0), DEAD, 0.0)
            block_ref[start : start + capacity, :LANES] = (block[:, :LANES] + mark).astype(jnp.bfloat16)
            block_ref[start : start + capacity, LANES:] = block[:, LANES:].astype(jnp.bfloat16)
            done += capacity


def pack(cluster_row, embeddings, first_block, block_counts, clusters, capacity, mixed):
    rows, width = embeddings.shape
    steps = 3 if rows % 384 == 0 else 1
    total = sum(block_counts) * capacity
    vmem = pl.BlockSpec(memory_space=pltpu.VMEM)
    *blocks, slots = pl.pallas_call(
        functools.partial(pack_kernel, first_block, mixed, clusters, capacity),
        in_specs=[vmem, pl.BlockSpec(memory_space=pltpu.HBM)],
        out_specs=[vmem] * (len(block_counts) + 1),
        out_shape=[jax.ShapeDtypeStruct((count * capacity, width), jnp.bfloat16) for count in block_counts]
        + [jax.ShapeDtypeStruct((1, rows), jnp.int32)],
        scratch_shapes=[
            pltpu.VMEM((steps, rows // steps, width), jnp.float32),
            pltpu.VMEM((rows, width), jnp.bfloat16),
            pltpu.VMEM((total, rows), jnp.bfloat16),
            pltpu.SemaphoreType.DMA((steps,)),
        ],
        compiler_params=pltpu.CompilerParams(vmem_limit_bytes=VMEM_LIMIT),
        cost_estimate=pl.CostEstimate(
            flops=2 * total * rows * width, bytes_accessed=rows * width * 4 + total * width * 2, transcendentals=rows
        ),
    )(cluster_row, embeddings)
    return blocks, slots


def pieces(refs, tile):
    groups, current, held = [], [], 0
    for ref in refs:
        start = 0
        while start < ref.shape[0]:
            size = min(tile - held, ref.shape[0] - start)
            current.append((ref, start, size))
            start += size
            held += size
            if held == tile:
                groups.append(current)
                current, held = [], 0
    if current:
        groups.append(current)
    return groups


def load(group):
    parts = [ref[start : start + size, :] for ref, start, size in group]
    return parts[0] if len(parts) == 1 else jnp.concatenate(parts, axis=0)


def tile_best(key, query, shift):
    deep, wide = key.shape[0], query.shape[0]
    scores = lax.dot_general(key, query, (((1,), (1,)), ((), ())), preferred_element_type=jnp.float32)
    dead = key[:, :1].astype(jnp.float32) > 2.0
    scores = scores + jnp.where(dead, 2 * FLOOR, 0.0)
    if shift is not None and -wide < shift < deep:
        own = lax.broadcasted_iota(jnp.int32, scores.shape, 0) == (
            lax.broadcasted_iota(jnp.int32, scores.shape, 1) + shift
        )
        scores = jnp.where(own, FLOOR, scores)
    return jnp.max(scores.reshape(deep // 8, 8, wide), axis=0)


def score_kernel(n_own, n_other, n_old, mixed, *refs):
    own_refs = refs[:n_own]
    other_refs = refs[n_own : n_own + n_other]
    start_ref = refs[n_own + n_other] if n_old else None
    best_ref = refs[-1]
    per_ref = own_refs[0].shape[0] // LANES
    chip = lax.axis_index("owners") // 2 if mixed else 0

    def run(query_refs, query_first, key_sets, has_start):
        at = query_first
        for query_group in pieces(query_refs, 256):
            query = load(query_group)
            wide = query.shape[0]
            best = jnp.full((8, wide), FLOOR, jnp.float32)
            for key_refs, key_first in key_sets:
                for key_group in pieces(key_refs, 512):
                    key = load(key_group)
                    best = jnp.maximum(best, tile_best(key, query, None if key_first is None else at - key_first))
                    if key_first is not None:
                        key_first += key.shape[0]
            row = jnp.max(best, axis=0, keepdims=True)
            for lane in range(0, wide, LANES):
                index = (at + lane) // LANES
                part = row[:, lane : lane + LANES]
                if has_start:
                    part = jnp.maximum(part, start_ref[index : index + 1, :])
                best_ref[pl.ds(lax.bitwise_xor(index, chip) if mixed else index, 1), :] = part
            at += wide

    old = n_old * per_ref * LANES
    if n_old:
        run(own_refs[:n_old], 0, [(own_refs[n_old:], old), (other_refs[n_old:], None)], True)
    run(own_refs[n_old:], old, [(own_refs, 0), (other_refs, None)], False)


def score(own, other, n_old=0, start=None, mixed=False):
    n_own = sum(block.shape[0] for block in own)
    n_key = n_own + sum(block.shape[0] for block in other)
    width = own[0].shape[1]
    args = [*own, *other] + ([] if start is None else [start])
    return pl.pallas_call(
        functools.partial(score_kernel, len(own), len(other), n_old, mixed),
        in_specs=[pl.BlockSpec(memory_space=pltpu.VMEM)] * len(args),
        out_specs=pl.BlockSpec(memory_space=pltpu.VMEM),
        out_shape=jax.ShapeDtypeStruct((n_own // LANES, LANES), jnp.float32),
        compiler_params=pltpu.CompilerParams(vmem_limit_bytes=VMEM_LIMIT),
        cost_estimate=pl.CostEstimate(
            flops=2 * n_own * n_key * width, bytes_accessed=n_key * width * 2, transcendentals=0
        ),
    )(*args)


def lookup_kernel(capacity, mixed, slot_ref, answer_ref, out_ref):
    slots = slot_ref[...]
    clusters = answer_ref.shape[0]
    shift = capacity.bit_length() - 1
    place = lax.bitwise_and(slots, capacity - 1)
    which = lax.shift_right_logical(slots, shift)
    if mixed:
        which = lax.bitwise_xor(which, lax.axis_index("owners") // 2)
    rows = slots.shape[1]
    pick = (lax.broadcasted_iota(jnp.int32, (capacity, rows), 0) == place).astype(jnp.float32).astype(jnp.bfloat16)
    rest = answer_ref[...]
    total = jnp.zeros((clusters, rows), jnp.float32)
    for _ in range(3):
        part = rest.astype(jnp.bfloat16)
        rest = rest - part.astype(jnp.float32)
        total = total + jnp.dot(part, pick, preferred_element_type=jnp.float32)
    mine = lax.broadcasted_iota(jnp.int32, (clusters, rows), 0) == which
    found = jnp.sum(jnp.where(mine, total, 0.0), axis=0, keepdims=True)
    out_ref[...] = jnp.maximum(found, -1.0).reshape(out_ref.shape)


def lookup(slots, answers, capacity, mixed):
    return pl.pallas_call(
        functools.partial(lookup_kernel, capacity, mixed),
        in_specs=[pl.BlockSpec(memory_space=pltpu.VMEM)] * 2,
        out_specs=pl.BlockSpec(memory_space=pltpu.VMEM),
        out_shape=jax.ShapeDtypeStruct((slots.shape[1],), jnp.float32),
        compiler_params=pltpu.CompilerParams(vmem_limit_bytes=VMEM_LIMIT),
    )(slots, answers)


def by_xor(value, axis, mask):
    return lax.ppermute(value, axis, [(source, source ^ mask) for source in range(lax.axis_size(axis))])


def after(value, *before):
    return lax.optimization_barrier((value, *before))[0]


def on_device(embeddings, cluster_of):
    owners = lax.axis_size("owners")
    clusters = owners // 2
    capacity = SLOTS // clusters
    rows = embeddings.shape[0]
    cluster_row = cluster_of.reshape(1, rows)
    same_core = [list(range(core, owners, 2)) for core in range(2)]
    mixed = clusters == 8
    if mixed:
        send = lambda block, mask: by_xor(block, "owners", 2 * mask)
        swap = lambda block: by_xor(block, "owners", 1)
        (out4, out5), slots = pack(cluster_row, embeddings, 4, [1, 1], clusters, capacity, mixed)
        far4, far5 = send(out4, 4), send(out5, 5)
        (own, out1, out2, out3), _ = pack(cluster_row, embeddings, 0, [1] * 4, clusters, capacity, mixed)
        (out6, out7), _ = pack(cluster_row, embeddings, 6, [1] * 2, clusters, capacity, mixed)
        near = [own, send(out1, 1), send(out2, 2), send(out3, 3)]
        far6 = send(after(out6, far4), 6)
        far7 = send(after(out7, far5), 7)
        early = [*near, far4, far5]
        early_other = [swap(block) for block in early]
        early_best = score(early, early_other)
        late = [far6, after(far7, early_best)]
        late_other = [swap(block) for block in late]
        best = score(early + late, early_other + late_other, 6, early_best, mixed)
    else:
        (outgoing,), slots = pack(cluster_row, embeddings, 0, [clusters], clusters, capacity, mixed)
        own = lax.all_to_all(
            outgoing.reshape(clusters, capacity, -1), "owners", 0, 0, axis_index_groups=same_core, tiled=True
        ).reshape(SLOTS, -1)
        best = score([own], [by_xor(own, "owners", 1)]).reshape(clusters, capacity)
    answers = lax.all_to_all(best, "owners", 0, 0, axis_index_groups=same_core, tiled=True)
    return lookup(slots, answers, capacity, mixed)


def solution(mesh):
    placed = (P(("groups", "owners"), None), P(("groups", "owners")))
    return jax.shard_map(
        on_device, mesh=mesh, in_specs=placed, out_specs=P(("groups", "owners")), check_vma=False
    )
```

```python
import functools

import jax
import jax.numpy as jnp
from jax import lax
from jax.experimental import pallas as pl
from jax.experimental.pallas import tpu as pltpu
from jax.sharding import PartitionSpec as P

SLOTS = 1024
FLOOR = -4.0
DEAD = 4.0
VMEM_LIMIT = 40 * 2**20
LANES = 128


def row_slots(relative, clusters, capacity):
    rows = relative.shape[1]
    ids = lax.broadcasted_iota(jnp.int32, (clusters, LANES), 0)
    earlier = (
        lax.broadcasted_iota(jnp.int32, (LANES, LANES), 0)
        < lax.broadcasted_iota(jnp.int32, (LANES, LANES), 1)
    ).astype(jnp.bfloat16)
    carry = jnp.zeros((clusters, 1), jnp.float32)
    places = []
    for first in range(0, rows, LANES):
        part = relative[:, first : first + LANES]
        member = (ids == part).astype(jnp.float32)
        before = carry + jnp.dot(
            member.astype(jnp.bfloat16), earlier, preferred_element_type=jnp.float32
        )
        place = jnp.sum(before * member, axis=0, keepdims=True)
        places.append(part * capacity + place.astype(jnp.int32))
        carry = carry + jnp.sum(member, axis=1, keepdims=True)
    return jnp.concatenate(places, axis=1), carry


def picks(slots, taken, capacity, pick_ref):
    done = 0
    for first, count in taken:
        size = count * capacity
        wanted = lax.broadcasted_iota(jnp.int32, (size, slots.shape[1]), 0) + first * capacity
        pick_ref[done : done + size, :] = (wanted == slots).astype(jnp.float32).astype(jnp.bfloat16)
        done += size


def select(taken, capacity, counts, pick_ref, unit_ref, block_refs):
    lane = lax.broadcasted_iota(jnp.int32, (capacity, LANES), 1)
    place = lax.broadcasted_iota(jnp.int32, (capacity, LANES), 0).astype(jnp.float32)
    done = 0
    for block_ref, (first, count) in zip(block_refs, taken):
        for index in range(count):
            block = jnp.dot(
                pick_ref[done : done + capacity, :], unit_ref[...], preferred_element_type=jnp.float32
            )
            full = counts[first + index : first + index + 1, :]
            mark = jnp.where((place >= full) & (lane == 0), DEAD, 0.0)
            start = index * capacity
            block_ref[start : start + capacity, :LANES] = (block[:, :LANES] + mark).astype(jnp.bfloat16)
            block_ref[start : start + capacity, LANES:] = block[:, LANES:].astype(jnp.bfloat16)
            done += capacity


def pack_kernel(taken, mixed, clusters, capacity, cluster_ref, rows_ref, *refs):
    *block_refs, slot_ref, count_ref, unit_ref, ids_ref, held_ref, pick_ref, sems = refs
    steps, tile, _ = held_ref.shape
    ids_copy = pltpu.make_async_copy(cluster_ref, ids_ref, sems.at[steps])
    ids_copy.start()
    copies = [
        pltpu.make_async_copy(rows_ref.at[pl.ds(step * tile, tile), :], held_ref.at[step], sems.at[step])
        for step in range(steps)
    ]
    for copy in copies:
        copy.start()
    ids_copy.wait()
    relative = ids_ref[...].reshape(1, steps * tile)
    if mixed:
        relative = lax.bitwise_xor(relative, lax.axis_index("owners") // 2)
    slots, counts = row_slots(relative, clusters, capacity)
    slot_ref[...] = slots
    count_ref[...] = jnp.broadcast_to(counts, count_ref.shape)
    picks(slots, taken, capacity, pick_ref)
    for step, copy in enumerate(copies):
        copy.wait()
        values = held_ref[step]
        scale = lax.rsqrt(jnp.sum(values * values, axis=1, keepdims=True) + 1e-06)
        unit_ref[step * tile : (step + 1) * tile, :] = (values * scale).astype(jnp.bfloat16)
    select(taken, capacity, counts, pick_ref, unit_ref, block_refs)


def pack_cost(taken, capacity, rows, width):
    total = sum(count for _, count in taken) * capacity
    return pl.CostEstimate(
        flops=2 * total * rows * width, bytes_accessed=rows * width * 4 + total * width * 2, transcendentals=rows
    )


def block_shapes(taken, capacity, width):
    return [jax.ShapeDtypeStruct((count * capacity, width), jnp.bfloat16) for _, count in taken]


def pack(cluster_of, embeddings, taken, clusters, capacity, mixed):
    rows, width = embeddings.shape
    steps = 3 if rows % 384 == 0 else 1
    total = sum(count for _, count in taken) * capacity
    vmem = pl.BlockSpec(memory_space=pltpu.VMEM)
    *blocks, slots, counts, unit = pl.pallas_call(
        functools.partial(pack_kernel, taken, mixed, clusters, capacity),
        in_specs=[pl.BlockSpec(memory_space=pl.ANY)] * 2,
        out_specs=[vmem] * (len(taken) + 3),
        out_shape=block_shapes(taken, capacity, width)
        + [
            jax.ShapeDtypeStruct((1, rows), jnp.int32),
            jax.ShapeDtypeStruct((clusters, LANES), jnp.float32),
            jax.ShapeDtypeStruct((rows, width), jnp.bfloat16),
        ],
        scratch_shapes=[
            pltpu.VMEM((rows,), jnp.int32),
            pltpu.VMEM((steps, rows // steps, width), jnp.float32),
            pltpu.VMEM((total, rows), jnp.bfloat16),
            pltpu.SemaphoreType.DMA((steps + 1,)),
        ],
        compiler_params=pltpu.CompilerParams(vmem_limit_bytes=VMEM_LIMIT),
        cost_estimate=pack_cost(taken, capacity, rows, width),
    )(
        pltpu.with_memory_space_constraint(cluster_of, pltpu.HBM),
        pltpu.with_memory_space_constraint(embeddings, pltpu.HBM),
    )
    return blocks, (slots, counts, unit)


def more_kernel(taken, capacity, slot_ref, count_ref, unit_ref, *refs):
    *block_refs, pick_ref = refs
    picks(slot_ref[...], taken, capacity, pick_ref)
    select(taken, capacity, count_ref[...], pick_ref, unit_ref, block_refs)


def pack_more(packed, taken, capacity):
    rows, width = packed[2].shape
    total = sum(count for _, count in taken) * capacity
    vmem = pl.BlockSpec(memory_space=pltpu.VMEM)
    return pl.pallas_call(
        functools.partial(more_kernel, taken, capacity),
        in_specs=[vmem] * 3,
        out_specs=[vmem] * len(taken),
        out_shape=block_shapes(taken, capacity, width),
        scratch_shapes=[pltpu.VMEM((total, rows), jnp.bfloat16)],
        compiler_params=pltpu.CompilerParams(vmem_limit_bytes=VMEM_LIMIT),
        cost_estimate=pack_cost(taken, capacity, rows, width),
    )(*packed)


def pieces(refs, tile):
    groups, current, held = [], [], 0
    for ref in refs:
        start = 0
        while start < ref.shape[0]:
            size = min(tile - held, ref.shape[0] - start)
            current.append((ref, start, size))
            start += size
            held += size
            if held == tile:
                groups.append(current)
                current, held = [], 0
    if current:
        groups.append(current)
    return groups


def load(group):
    parts = [ref[start : start + size, :] for ref, start, size in group]
    return parts[0] if len(parts) == 1 else jnp.concatenate(parts, axis=0)


def tile_best(key, query, shift):
    deep, wide = key.shape[0], query.shape[0]
    scores = lax.dot_general(key, query, (((1,), (1,)), ((), ())), preferred_element_type=jnp.float32)
    dead = key[:, :1].astype(jnp.float32) > 2.0
    scores = scores + jnp.where(dead, 2 * FLOOR, 0.0)
    if shift is not None and -wide < shift < deep:
        own = lax.broadcasted_iota(jnp.int32, scores.shape, 0) == (
            lax.broadcasted_iota(jnp.int32, scores.shape, 1) + shift
        )
        scores = jnp.where(own, FLOOR, scores)
    return jnp.max(scores.reshape(deep // 8, 8, wide), axis=0)


def score_kernel(plan, n_blocks, has_start, order, *refs):
    start_ref = refs[n_blocks] if has_start else None
    best_ref = refs[-1]
    chip = lax.axis_index("owners") // 2 if order else 0
    at = 0
    for query_block, key_blocks, starts in plan:
        first = 0
        for query_group in pieces([refs[query_block]], 256):
            query = load(query_group)
            wide = query.shape[0]
            best = jnp.full((8, wide), FLOOR, jnp.float32)
            for key_block in key_blocks:
                key_first = 0
                for key_group in pieces([refs[key_block]], 512):
                    key = load(key_group)
                    shift = first - key_first if key_block == query_block else None
                    best = jnp.maximum(best, tile_best(key, query, shift))
                    key_first += key.shape[0]
            row = jnp.max(best, axis=0, keepdims=True)
            for lane in range(0, wide, LANES):
                index = (at + first + lane) // LANES
                part = row[:, lane : lane + LANES]
                if starts:
                    part = jnp.maximum(part, start_ref[index : index + 1, :])
                best_ref[pl.ds(lax.bitwise_xor(order[index], chip) if order else index, 1), :] = part
            first += wide
        at += first


def score(blocks, plan, start=None, order=None):
    n_query = sum(blocks[query].shape[0] for query, _, _ in plan)
    pairs = sum(blocks[query].shape[0] * blocks[key].shape[0] for query, keys, _ in plan for key in keys)
    width = blocks[0].shape[1]
    args = [*blocks] + ([] if start is None else [start])
    return pl.pallas_call(
        functools.partial(score_kernel, plan, len(blocks), start is not None, order),
        in_specs=[pl.BlockSpec(memory_space=pltpu.VMEM)] * len(args),
        out_specs=pl.BlockSpec(memory_space=pltpu.VMEM),
        out_shape=jax.ShapeDtypeStruct((n_query // LANES, LANES), jnp.float32),
        compiler_params=pltpu.CompilerParams(vmem_limit_bytes=VMEM_LIMIT),
        cost_estimate=pl.CostEstimate(
            flops=2 * pairs * width,
            bytes_accessed=sum(block.size for block in blocks) * 2,
            transcendentals=0,
        ),
    )(*args)


def lookup_kernel(capacity, mixed, slot_ref, answer_ref, out_ref):
    slots = slot_ref[...]
    clusters = answer_ref.shape[0]
    shift = capacity.bit_length() - 1
    place = lax.bitwise_and(slots, capacity - 1)
    which = lax.shift_right_logical(slots, shift)
    if mixed:
        which = lax.bitwise_xor(which, lax.axis_index("owners") // 2)
    rows = slots.shape[1]
    pick = (lax.broadcasted_iota(jnp.int32, (capacity, rows), 0) == place).astype(jnp.float32).astype(jnp.bfloat16)
    rest = answer_ref[...]
    total = jnp.zeros((clusters, rows), jnp.float32)
    for _ in range(3):
        part = rest.astype(jnp.bfloat16)
        rest = rest - part.astype(jnp.float32)
        total = total + jnp.dot(part, pick, preferred_element_type=jnp.float32)
    mine = lax.broadcasted_iota(jnp.int32, (clusters, rows), 0) == which
    found = jnp.sum(jnp.where(mine, total, 0.0), axis=0, keepdims=True)
    out_ref[...] = jnp.maximum(found, -1.0).reshape(out_ref.shape)


def lookup(slots, answers, capacity, mixed):
    return pl.pallas_call(
        functools.partial(lookup_kernel, capacity, mixed),
        in_specs=[pl.BlockSpec(memory_space=pltpu.VMEM)] * 2,
        out_specs=pl.BlockSpec(memory_space=pltpu.VMEM),
        out_shape=jax.ShapeDtypeStruct((slots.shape[1],), jnp.float32),
        compiler_params=pltpu.CompilerParams(vmem_limit_bytes=VMEM_LIMIT),
    )(slots, answers)


def by_xor(value, axis, mask):
    return lax.ppermute(value, axis, [(source, source ^ mask) for source in range(lax.axis_size(axis))])


def after(value, *before):
    return lax.optimization_barrier((value, *before))[0]


def on_device(embeddings, cluster_of):
    owners = lax.axis_size("owners")
    clusters = owners // 2
    capacity = SLOTS // clusters
    same_core = [list(range(core, owners, 2)) for core in range(2)]
    mixed = clusters == 8
    if mixed:
        send = lambda block, mask: by_xor(block, "owners", 2 * mask)
        swap = lambda block: by_xor(block, "owners", 1)
        first, then = (4, 5), (0, 1, 2, 3, 6, 7)
        blocks = {}
        got, packed = pack(cluster_of, embeddings, [(index, 1) for index in first], clusters, capacity, mixed)
        blocks.update(zip(first, got))
        blocks.update(zip(then, pack_more(packed, [(index, 1) for index in then], capacity)))
        waits = {6: (4,), 7: (5,)}
        have = {0: blocks[0]}
        for index in (4, 5, 1, 2, 3, 6, 7):
            have[index] = send(after(blocks[index], *[have[wait] for wait in waits.get(index, ())]), index)
        early = jnp.concatenate([have[index] for index in [0, 4, 5, 1]], axis=0)
        early_other = swap(early)
        best = score([early, early_other], [(0, [0, 1], False)])
        late = jnp.concatenate([have[index] for index in [2, 3, 6, 7]], axis=0)
        late_other = swap(late)
        best = score([early, late], [(0, [1], True), (1, [0, 1], False)], best)
        best = score(
            [early, late, early_other, late_other], [(0, [3], True), (1, [2, 3], True)], best, [0, 4, 5, 1, 2, 3, 6, 7]
        )
        slots = packed[0]
    else:
        (outgoing,), (slots, _, _) = pack(cluster_of, embeddings, [(0, clusters)], clusters, capacity, mixed)
        own = lax.all_to_all(
            outgoing.reshape(clusters, capacity, -1), "owners", 0, 0, axis_index_groups=same_core, tiled=True
        ).reshape(SLOTS, -1)
        other = by_xor(own, "owners", 1)
        best = score([own], [(0, [0], False)])
        best = score([own, other], [(0, [1], True)], best).reshape(clusters, capacity)
    answers = lax.all_to_all(best, "owners", 0, 0, axis_index_groups=same_core, tiled=True)
    return lookup(slots, answers, capacity, mixed)


def solution(mesh):
    placed = (P(("groups", "owners"), None), P(("groups", "owners")))
    return jax.shard_map(
        on_device, mesh=mesh, in_specs=placed, out_specs=P(("groups", "owners")), check_vma=False
    )
```

```python
import functools

import jax
import jax.numpy as jnp
from jax import lax
from jax.experimental import pallas as pl
from jax.experimental.pallas import tpu as pltpu
from jax.sharding import PartitionSpec as P

SLOTS = 1024
FLOOR = -4.0
DEAD = 4.0
VMEM_LIMIT = 40 * 2**20
LANES = 128


def row_slots(relative, clusters, capacity):
    rows = relative.shape[1]
    ids = lax.broadcasted_iota(jnp.int32, (clusters, LANES), 0)
    earlier = (
        lax.broadcasted_iota(jnp.int32, (LANES, LANES), 0)
        < lax.broadcasted_iota(jnp.int32, (LANES, LANES), 1)
    ).astype(jnp.bfloat16)
    carry = jnp.zeros((clusters, 1), jnp.float32)
    places = []
    for first in range(0, rows, LANES):
        part = relative[:, first : first + LANES]
        member = (ids == part).astype(jnp.float32)
        before = carry + jnp.dot(
            member.astype(jnp.bfloat16), earlier, preferred_element_type=jnp.float32
        )
        place = jnp.sum(before * member, axis=0, keepdims=True)
        places.append(part * capacity + place.astype(jnp.int32))
        carry = carry + jnp.sum(member, axis=1, keepdims=True)
    return jnp.concatenate(places, axis=1), carry


def picks(slots, taken, capacity, pick_ref):
    done = 0
    for first, count in taken:
        size = count * capacity
        wanted = lax.broadcasted_iota(jnp.int32, (size, slots.shape[1]), 0) + first * capacity
        pick_ref[done : done + size, :] = (wanted == slots).astype(jnp.float32).astype(jnp.bfloat16)
        done += size


def select(taken, capacity, counts, pick_ref, unit_ref, block_refs):
    lane = lax.broadcasted_iota(jnp.int32, (capacity, LANES), 1)
    place = lax.broadcasted_iota(jnp.int32, (capacity, LANES), 0).astype(jnp.float32)
    done = 0
    for block_ref, (first, count) in zip(block_refs, taken):
        for index in range(count):
            block = jnp.dot(
                pick_ref[done : done + capacity, :], unit_ref[...], preferred_element_type=jnp.float32
            )
            full = counts[first + index : first + index + 1, :]
            mark = jnp.where((place >= full) & (lane == 0), DEAD, 0.0)
            start = index * capacity
            block_ref[start : start + capacity, :LANES] = (block[:, :LANES] + mark).astype(jnp.bfloat16)
            block_ref[start : start + capacity, LANES:] = block[:, LANES:].astype(jnp.bfloat16)
            done += capacity


def pack_kernel(taken, mixed, clusters, capacity, cluster_ref, rows_ref, *refs):
    *block_refs, slot_ref, count_ref, unit_ref, ids_ref, held_ref, pick_ref, sems = refs
    steps, tile, _ = held_ref.shape
    ids_copy = pltpu.make_async_copy(cluster_ref, ids_ref, sems.at[steps])
    ids_copy.start()
    copies = [
        pltpu.make_async_copy(rows_ref.at[pl.ds(step * tile, tile), :], held_ref.at[step], sems.at[step])
        for step in range(steps)
    ]
    for copy in copies:
        copy.start()
    ids_copy.wait()
    relative = ids_ref[...].reshape(1, steps * tile)
    if mixed:
        relative = lax.bitwise_xor(relative, lax.axis_index("owners") // 2)
    slots, counts = row_slots(relative, clusters, capacity)
    slot_ref[...] = slots
    count_ref[...] = jnp.broadcast_to(counts, count_ref.shape)
    picks(slots, taken, capacity, pick_ref)
    for step, copy in enumerate(copies):
        copy.wait()
        values = held_ref[step]
        scale = lax.rsqrt(jnp.sum(values * values, axis=1, keepdims=True) + 1e-06)
        unit_ref[step * tile : (step + 1) * tile, :] = (values * scale).astype(jnp.bfloat16)
    select(taken, capacity, counts, pick_ref, unit_ref, block_refs)


def pack_cost(taken, capacity, rows, width):
    total = sum(count for _, count in taken) * capacity
    return pl.CostEstimate(
        flops=2 * total * rows * width, bytes_accessed=rows * width * 4 + total * width * 2, transcendentals=rows
    )


def block_shapes(taken, capacity, width):
    return [jax.ShapeDtypeStruct((count * capacity, width), jnp.bfloat16) for _, count in taken]


def pack(cluster_of, embeddings, taken, clusters, capacity, mixed):
    rows, width = embeddings.shape
    steps = 3 if rows % 384 == 0 else 1
    total = sum(count for _, count in taken) * capacity
    vmem = pl.BlockSpec(memory_space=pltpu.VMEM)
    *blocks, slots, counts, unit = pl.pallas_call(
        functools.partial(pack_kernel, taken, mixed, clusters, capacity),
        in_specs=[pl.BlockSpec(memory_space=pl.ANY)] * 2,
        out_specs=[vmem] * (len(taken) + 3),
        out_shape=block_shapes(taken, capacity, width)
        + [
            jax.ShapeDtypeStruct((1, rows), jnp.int32),
            jax.ShapeDtypeStruct((clusters, LANES), jnp.float32),
            jax.ShapeDtypeStruct((rows, width), jnp.bfloat16),
        ],
        scratch_shapes=[
            pltpu.VMEM((rows,), jnp.int32),
            pltpu.VMEM((steps, rows // steps, width), jnp.float32),
            pltpu.VMEM((total, rows), jnp.bfloat16),
            pltpu.SemaphoreType.DMA((steps + 1,)),
        ],
        compiler_params=pltpu.CompilerParams(vmem_limit_bytes=VMEM_LIMIT),
        cost_estimate=pack_cost(taken, capacity, rows, width),
    )(
        pltpu.with_memory_space_constraint(cluster_of, pltpu.HBM),
        pltpu.with_memory_space_constraint(embeddings, pltpu.HBM),
    )
    return blocks, (slots, counts, unit)


def more_kernel(taken, capacity, slot_ref, count_ref, unit_ref, *refs):
    *block_refs, pick_ref = refs
    picks(slot_ref[...], taken, capacity, pick_ref)
    select(taken, capacity, count_ref[...], pick_ref, unit_ref, block_refs)


def pack_more(packed, taken, capacity):
    rows, width = packed[2].shape
    total = sum(count for _, count in taken) * capacity
    vmem = pl.BlockSpec(memory_space=pltpu.VMEM)
    return pl.pallas_call(
        functools.partial(more_kernel, taken, capacity),
        in_specs=[vmem] * 3,
        out_specs=[vmem] * len(taken),
        out_shape=block_shapes(taken, capacity, width),
        scratch_shapes=[pltpu.VMEM((total, rows), jnp.bfloat16)],
        compiler_params=pltpu.CompilerParams(vmem_limit_bytes=VMEM_LIMIT),
        cost_estimate=pack_cost(taken, capacity, rows, width),
    )(*packed)


def pieces(refs, tile):
    groups, current, held = [], [], 0
    for ref in refs:
        start = 0
        while start < ref.shape[0]:
            size = min(tile - held, ref.shape[0] - start)
            current.append((ref, start, size))
            start += size
            held += size
            if held == tile:
                groups.append(current)
                current, held = [], 0
    if current:
        groups.append(current)
    return groups


def load(group):
    parts = [ref[start : start + size, :] for ref, start, size in group]
    return parts[0] if len(parts) == 1 else jnp.concatenate(parts, axis=0)


def tile_best(key, query, shift):
    deep, wide = key.shape[0], query.shape[0]
    scores = lax.dot_general(key, query, (((1,), (1,)), ((), ())), preferred_element_type=jnp.float32)
    dead = key[:, :1].astype(jnp.float32) > 2.0
    scores = scores + jnp.where(dead, 2 * FLOOR, 0.0)
    if shift is not None and -wide < shift < deep:
        own = lax.broadcasted_iota(jnp.int32, scores.shape, 0) == (
            lax.broadcasted_iota(jnp.int32, scores.shape, 1) + shift
        )
        scores = jnp.where(own, FLOOR, scores)
    return jnp.max(scores.reshape(deep // 8, 8, wide), axis=0)


def score_kernel(plan, n_blocks, has_start, order, *refs):
    start_ref = refs[n_blocks] if has_start else None
    best_ref = refs[-1]
    chip = lax.axis_index("owners") // 2 if order else 0
    at = 0
    for query_blocks, key_blocks, starts in plan:
        first = 0
        for query_group in pieces([refs[block] for block in query_blocks], 256):
            query = load(query_group)
            wide = query.shape[0]
            best = jnp.full((8, wide), FLOOR, jnp.float32)
            for key_block in key_blocks:
                key_first = 0
                for key_group in pieces([refs[key_block]], 512):
                    key = load(key_group)
                    shift = first - key_first if (key_block,) == query_blocks else None
                    best = jnp.maximum(best, tile_best(key, query, shift))
                    key_first += key.shape[0]
            row = jnp.max(best, axis=0, keepdims=True)
            for lane in range(0, wide, LANES):
                index = (at + first + lane) // LANES
                part = row[:, lane : lane + LANES]
                if starts:
                    part = jnp.maximum(part, start_ref[index : index + 1, :])
                best_ref[pl.ds(lax.bitwise_xor(order[index], chip) if order else index, 1), :] = part
            first += wide
        at += first


def score(blocks, plan, start=None, order=None):
    n_query = sum(blocks[query].shape[0] for queries, _, _ in plan for query in queries)
    pairs = sum(
        blocks[query].shape[0] * blocks[key].shape[0] for queries, keys, _ in plan for query in queries for key in keys
    )
    width = blocks[0].shape[1]
    args = [*blocks] + ([] if start is None else [start])
    return pl.pallas_call(
        functools.partial(score_kernel, plan, len(blocks), start is not None, order),
        in_specs=[pl.BlockSpec(memory_space=pltpu.VMEM)] * len(args),
        out_specs=pl.BlockSpec(memory_space=pltpu.VMEM),
        out_shape=jax.ShapeDtypeStruct((n_query // LANES, LANES), jnp.float32),
        compiler_params=pltpu.CompilerParams(vmem_limit_bytes=VMEM_LIMIT),
        cost_estimate=pl.CostEstimate(
            flops=2 * pairs * width,
            bytes_accessed=sum(block.size for block in blocks) * 2,
            transcendentals=0,
        ),
    )(*args)


def lookup_kernel(capacity, mixed, slot_ref, answer_ref, out_ref):
    slots = slot_ref[...]
    clusters = answer_ref.shape[0]
    shift = capacity.bit_length() - 1
    place = lax.bitwise_and(slots, capacity - 1)
    which = lax.shift_right_logical(slots, shift)
    if mixed:
        which = lax.bitwise_xor(which, lax.axis_index("owners") // 2)
    rows = slots.shape[1]
    pick = (lax.broadcasted_iota(jnp.int32, (capacity, rows), 0) == place).astype(jnp.float32).astype(jnp.bfloat16)
    rest = answer_ref[...]
    total = jnp.zeros((clusters, rows), jnp.float32)
    for _ in range(3):
        part = rest.astype(jnp.bfloat16)
        rest = rest - part.astype(jnp.float32)
        total = total + jnp.dot(part, pick, preferred_element_type=jnp.float32)
    mine = lax.broadcasted_iota(jnp.int32, (clusters, rows), 0) == which
    found = jnp.sum(jnp.where(mine, total, 0.0), axis=0, keepdims=True)
    out_ref[...] = jnp.maximum(found, -1.0).reshape(out_ref.shape)


def lookup(slots, answers, capacity, mixed):
    return pl.pallas_call(
        functools.partial(lookup_kernel, capacity, mixed),
        in_specs=[pl.BlockSpec(memory_space=pltpu.VMEM)] * 2,
        out_specs=pl.BlockSpec(memory_space=pltpu.VMEM),
        out_shape=jax.ShapeDtypeStruct((slots.shape[1],), jnp.float32),
        compiler_params=pltpu.CompilerParams(vmem_limit_bytes=VMEM_LIMIT),
    )(slots, answers)


def by_xor(value, axis, mask):
    return lax.ppermute(value, axis, [(source, source ^ mask) for source in range(lax.axis_size(axis))])


def after(value, *before):
    return lax.optimization_barrier((value, *before))[0]


def on_device(embeddings, cluster_of):
    owners = lax.axis_size("owners")
    clusters = owners // 2
    capacity = SLOTS // clusters
    same_core = [list(range(core, owners, 2)) for core in range(2)]
    mixed = clusters == 8
    if mixed:
        send = lambda block, mask: by_xor(block, "owners", 2 * mask)
        swap = lambda block: by_xor(block, "owners", 1)
        first, then = (4, 5), (0, 1, 2, 3, 6, 7)
        blocks = {}
        got, packed = pack(cluster_of, embeddings, [(index, 1) for index in first], clusters, capacity, mixed)
        blocks.update(zip(first, got))
        blocks.update(zip(then, pack_more(packed, [(index, 1) for index in then], capacity)))
        have = {0: blocks[0]}
        for index in (4, 5, 1, 2, 3):
            have[index] = send(blocks[index], index)
        have[6] = send(after(blocks[6], have[4]), 6)
        join = lambda *group: jnp.concatenate([have[index] for index in group], axis=0)
        early = join(0, 4, 5, 1)
        best = score([early], [((0,), [0], False)])
        have[7] = send(after(blocks[7], best), 7)
        early_other = swap(early)
        mid = join(2, 3, 6)
        best = score([early, mid], [((0,), [1], True), ((1,), [0, 1], False)], best)
        late = have[7] = after(have[7], best)
        near_other, late_other = swap(join(2, 3)), swap(join(6, 7))
        best = score([early, mid, late], [((0, 1), [2], True), ((2,), [0, 1, 2], False)], best)
        best = score([early, mid, late, early_other, near_other], [((0, 1, 2), [3, 4], True)], best)
        best = score(
            [early, mid, late, late_other], [((0, 1, 2), [3], True)], best, [0, 4, 5, 1, 2, 3, 6, 7]
        )
        slots = packed[0]
    else:
        (outgoing,), (slots, _, _) = pack(cluster_of, embeddings, [(0, clusters)], clusters, capacity, mixed)
        own = lax.all_to_all(
            outgoing.reshape(clusters, capacity, -1), "owners", 0, 0, axis_index_groups=same_core, tiled=True
        ).reshape(SLOTS, -1)
        other = by_xor(own, "owners", 1)
        best = score([own], [((0,), [0], False)])
        best = score([own, other], [((0,), [1], True)], best).reshape(clusters, capacity)
    answers = lax.all_to_all(best, "owners", 0, 0, axis_index_groups=same_core, tiled=True)
    return lookup(slots, answers, capacity, mixed)


def solution(mesh):
    placed = (P(("groups", "owners"), None), P(("groups", "owners")))
    return jax.shard_map(
        on_device, mesh=mesh, in_specs=placed, out_specs=P(("groups", "owners")), check_vma=False
    )
```

```python
import functools

import jax
import jax.numpy as jnp
from jax import lax
from jax.experimental import pallas as pl
from jax.experimental.pallas import tpu as pltpu
from jax.sharding import PartitionSpec as P

SLOTS = 1024
FLOOR = -4.0
DEAD = 4.0
VMEM_LIMIT = 40 * 2**20
LANES = 128


def row_slots(relative, clusters, capacity):
    rows = relative.shape[1]
    ids = lax.broadcasted_iota(jnp.int32, (clusters, LANES), 0)
    earlier = (
        lax.broadcasted_iota(jnp.int32, (LANES, LANES), 0)
        < lax.broadcasted_iota(jnp.int32, (LANES, LANES), 1)
    ).astype(jnp.bfloat16)
    carry = jnp.zeros((clusters, 1), jnp.float32)
    places = []
    for first in range(0, rows, LANES):
        part = relative[:, first : first + LANES]
        member = (ids == part).astype(jnp.float32)
        before = carry + jnp.dot(
            member.astype(jnp.bfloat16), earlier, preferred_element_type=jnp.float32
        )
        place = jnp.sum(before * member, axis=0, keepdims=True)
        places.append(part * capacity + place.astype(jnp.int32))
        carry = carry + jnp.sum(member, axis=1, keepdims=True)
    return jnp.concatenate(places, axis=1), carry


def picks(slots, taken, capacity, pick_ref):
    done = 0
    for first, count in taken:
        size = count * capacity
        wanted = lax.broadcasted_iota(jnp.int32, (size, slots.shape[1]), 0) + first * capacity
        pick_ref[done : done + size, :] = (wanted == slots).astype(jnp.float32).astype(jnp.bfloat16)
        done += size


def select(taken, capacity, counts, pick_ref, unit_ref, block_refs):
    lane = lax.broadcasted_iota(jnp.int32, (capacity, LANES), 1)
    place = lax.broadcasted_iota(jnp.int32, (capacity, LANES), 0).astype(jnp.float32)
    done = 0
    for block_ref, (first, count) in zip(block_refs, taken):
        for index in range(count):
            block = jnp.dot(
                pick_ref[done : done + capacity, :], unit_ref[...], preferred_element_type=jnp.float32
            )
            full = counts[first + index : first + index + 1, :]
            mark = jnp.where((place >= full) & (lane == 0), DEAD, 0.0)
            start = index * capacity
            block_ref[start : start + capacity, :LANES] = (block[:, :LANES] + mark).astype(jnp.bfloat16)
            block_ref[start : start + capacity, LANES:] = block[:, LANES:].astype(jnp.bfloat16)
            done += capacity


def pack_kernel(taken, mixed, clusters, capacity, cluster_ref, rows_ref, *refs):
    *block_refs, slot_ref, count_ref, unit_ref, ids_ref, held_ref, pick_ref, sems = refs
    steps, tile, _ = held_ref.shape
    ids_copy = pltpu.make_async_copy(cluster_ref, ids_ref, sems.at[steps])
    ids_copy.start()
    copies = [
        pltpu.make_async_copy(rows_ref.at[pl.ds(step * tile, tile), :], held_ref.at[step], sems.at[step])
        for step in range(steps)
    ]
    for copy in copies:
        copy.start()
    ids_copy.wait()
    relative = ids_ref[...].reshape(1, steps * tile)
    if mixed:
        relative = lax.bitwise_xor(relative, lax.axis_index("owners") // 2)
    slots, counts = row_slots(relative, clusters, capacity)
    slot_ref[...] = slots
    count_ref[...] = jnp.broadcast_to(counts, count_ref.shape)
    picks(slots, taken, capacity, pick_ref)
    for step, copy in enumerate(copies):
        copy.wait()
        values = held_ref[step]
        scale = lax.rsqrt(jnp.sum(values * values, axis=1, keepdims=True) + 1e-06)
        unit_ref[step * tile : (step + 1) * tile, :] = (values * scale).astype(jnp.bfloat16)
    select(taken, capacity, counts, pick_ref, unit_ref, block_refs)


def pack_cost(taken, capacity, rows, width):
    total = sum(count for _, count in taken) * capacity
    return pl.CostEstimate(
        flops=2 * total * rows * width, bytes_accessed=rows * width * 4 + total * width * 2, transcendentals=rows
    )


def block_shapes(taken, capacity, width):
    return [jax.ShapeDtypeStruct((count * capacity, width), jnp.bfloat16) for _, count in taken]


def pack(cluster_of, embeddings, taken, clusters, capacity, mixed):
    rows, width = embeddings.shape
    steps = 3 if rows % 384 == 0 else 1
    total = sum(count for _, count in taken) * capacity
    vmem = pl.BlockSpec(memory_space=pltpu.VMEM)
    *blocks, slots, counts, unit = pl.pallas_call(
        functools.partial(pack_kernel, taken, mixed, clusters, capacity),
        in_specs=[pl.BlockSpec(memory_space=pl.ANY)] * 2,
        out_specs=[vmem] * (len(taken) + 3),
        out_shape=block_shapes(taken, capacity, width)
        + [
            jax.ShapeDtypeStruct((1, rows), jnp.int32),
            jax.ShapeDtypeStruct((clusters, LANES), jnp.float32),
            jax.ShapeDtypeStruct((rows, width), jnp.bfloat16),
        ],
        scratch_shapes=[
            pltpu.VMEM((rows,), jnp.int32),
            pltpu.VMEM((steps, rows // steps, width), jnp.float32),
            pltpu.VMEM((total, rows), jnp.bfloat16),
            pltpu.SemaphoreType.DMA((steps + 1,)),
        ],
        compiler_params=pltpu.CompilerParams(vmem_limit_bytes=VMEM_LIMIT),
        cost_estimate=pack_cost(taken, capacity, rows, width),
    )(
        pltpu.with_memory_space_constraint(cluster_of, pltpu.HBM),
        pltpu.with_memory_space_constraint(embeddings, pltpu.HBM),
    )
    return blocks, (slots, counts, unit)


def more_kernel(taken, capacity, slot_ref, count_ref, unit_ref, *refs):
    *block_refs, pick_ref = refs
    picks(slot_ref[...], taken, capacity, pick_ref)
    select(taken, capacity, count_ref[...], pick_ref, unit_ref, block_refs)


def pack_more(packed, taken, capacity):
    rows, width = packed[2].shape
    total = sum(count for _, count in taken) * capacity
    vmem = pl.BlockSpec(memory_space=pltpu.VMEM)
    return pl.pallas_call(
        functools.partial(more_kernel, taken, capacity),
        in_specs=[vmem] * 3,
        out_specs=[vmem] * len(taken),
        out_shape=block_shapes(taken, capacity, width),
        scratch_shapes=[pltpu.VMEM((total, rows), jnp.bfloat16)],
        compiler_params=pltpu.CompilerParams(vmem_limit_bytes=VMEM_LIMIT),
        cost_estimate=pack_cost(taken, capacity, rows, width),
    )(*packed)


def pieces(refs, tile):
    groups, current, held = [], [], 0
    for ref in refs:
        start = 0
        while start < ref.shape[0]:
            size = min(tile - held, ref.shape[0] - start)
            current.append((ref, start, size))
            start += size
            held += size
            if held == tile:
                groups.append(current)
                current, held = [], 0
    if current:
        groups.append(current)
    return groups


def load(group):
    parts = [ref[start : start + size, :] for ref, start, size in group]
    return parts[0] if len(parts) == 1 else jnp.concatenate(parts, axis=0)


def own_rows(shape, key_group, query_group):
    found = None
    key_at = 0
    for key_ref, key_start, key_size in key_group:
        query_at = 0
        for query_ref, query_start, query_size in query_group:
            if key_ref is query_ref and key_start < query_start + query_size and query_start < key_start + key_size:
                row = lax.broadcasted_iota(jnp.int32, shape, 0)
                lane = lax.broadcasted_iota(jnp.int32, shape, 1)
                same = row - lane == query_start - query_at - key_start + key_at
                if key_size < shape[0]:
                    same = same & (row >= key_at) & (row < key_at + key_size)
                if query_size < shape[1]:
                    same = same & (lane >= query_at) & (lane < query_at + query_size)
                found = same if found is None else found | same
            query_at += query_size
        key_at += key_size
    return found


def tile_best(key_group, query_group, query):
    key = load(key_group)
    deep, wide = key.shape[0], query.shape[0]
    scores = lax.dot_general(key, query, (((1,), (1,)), ((), ())), preferred_element_type=jnp.float32)
    dead = key[:, :1].astype(jnp.float32) > 2.0
    scores = scores + jnp.where(dead, 2 * FLOOR, 0.0)
    own = own_rows(scores.shape, key_group, query_group)
    if own is not None:
        scores = jnp.where(own, FLOOR, scores)
    return jnp.max(scores.reshape(deep // 8, 8, wide), axis=0)


def score_kernel(plan, n_blocks, has_start, order, *refs):
    start_ref = refs[n_blocks] if has_start else None
    best_ref = refs[-1]
    chip = lax.axis_index("owners") // 2 if order else 0
    index = 0
    for query_blocks, key_blocks, starts in plan:
        for query_group in pieces([refs[block] for block in query_blocks], 256):
            query = load(query_group)
            best = jnp.full((8, query.shape[0]), FLOOR, jnp.float32)
            for key_group in pieces([refs[block] for block in key_blocks], 512):
                best = jnp.maximum(best, tile_best(key_group, query_group, query))
            row = jnp.max(best, axis=0, keepdims=True)
            for lane in range(0, query.shape[0], LANES):
                part = row[:, lane : lane + LANES]
                if starts:
                    part = jnp.maximum(part, start_ref[index : index + 1, :])
                best_ref[pl.ds(lax.bitwise_xor(order[index], chip) if order else index, 1), :] = part
                index += 1


def score(blocks, plan, start=None, order=None):
    n_query = sum(blocks[query].shape[0] for queries, _, _ in plan for query in queries)
    pairs = sum(
        blocks[query].shape[0] * blocks[key].shape[0] for queries, keys, _ in plan for query in queries for key in keys
    )
    width = blocks[0].shape[1]
    args = [*blocks] + ([] if start is None else [start])
    return pl.pallas_call(
        functools.partial(score_kernel, plan, len(blocks), start is not None, order),
        in_specs=[pl.BlockSpec(memory_space=pltpu.VMEM)] * len(args),
        out_specs=pl.BlockSpec(memory_space=pltpu.VMEM),
        out_shape=jax.ShapeDtypeStruct((n_query // LANES, LANES), jnp.float32),
        compiler_params=pltpu.CompilerParams(vmem_limit_bytes=VMEM_LIMIT),
        cost_estimate=pl.CostEstimate(
            flops=2 * pairs * width,
            bytes_accessed=sum(block.size for block in blocks) * 2,
            transcendentals=0,
        ),
    )(*args)


def lookup_kernel(capacity, mixed, slot_ref, answer_ref, out_ref):
    slots = slot_ref[...]
    clusters = answer_ref.shape[0]
    shift = capacity.bit_length() - 1
    place = lax.bitwise_and(slots, capacity - 1)
    which = lax.shift_right_logical(slots, shift)
    if mixed:
        which = lax.bitwise_xor(which, lax.axis_index("owners") // 2)
    rows = slots.shape[1]
    pick = (lax.broadcasted_iota(jnp.int32, (capacity, rows), 0) == place).astype(jnp.float32).astype(jnp.bfloat16)
    rest = answer_ref[...]
    total = jnp.zeros((clusters, rows), jnp.float32)
    for _ in range(3):
        part = rest.astype(jnp.bfloat16)
        rest = rest - part.astype(jnp.float32)
        total = total + jnp.dot(part, pick, preferred_element_type=jnp.float32)
    mine = lax.broadcasted_iota(jnp.int32, (clusters, rows), 0) == which
    found = jnp.sum(jnp.where(mine, total, 0.0), axis=0, keepdims=True)
    out_ref[...] = jnp.maximum(found, -1.0).reshape(out_ref.shape)


def lookup(slots, answers, capacity, mixed):
    return pl.pallas_call(
        functools.partial(lookup_kernel, capacity, mixed),
        in_specs=[pl.BlockSpec(memory_space=pltpu.VMEM)] * 2,
        out_specs=pl.BlockSpec(memory_space=pltpu.VMEM),
        out_shape=jax.ShapeDtypeStruct((slots.shape[1],), jnp.float32),
        compiler_params=pltpu.CompilerParams(vmem_limit_bytes=VMEM_LIMIT),
    )(slots, answers)


def by_xor(value, axis, mask):
    return lax.ppermute(value, axis, [(source, source ^ mask) for source in range(lax.axis_size(axis))])


def after(value, *before):
    return lax.optimization_barrier((value, *before))[0]


def on_device(embeddings, cluster_of):
    owners = lax.axis_size("owners")
    clusters = owners // 2
    capacity = SLOTS // clusters
    same_core = [list(range(core, owners, 2)) for core in range(2)]
    mixed = clusters == 8
    if mixed:
        send = lambda block, mask: by_xor(block, "owners", 2 * mask)
        swap = lambda block: by_xor(block, "owners", 1)
        first, then = (4, 5), (0, 1, 2, 3, 6, 7)
        blocks = {}
        got, packed = pack(cluster_of, embeddings, [(index, 1) for index in first], clusters, capacity, mixed)
        blocks.update(zip(first, got))
        blocks.update(zip(then, pack_more(packed, [(index, 1) for index in then], capacity)))
        have = {0: blocks[0]}
        for index in (4, 5, 1, 2, 3):
            have[index] = send(blocks[index], index)
        have[6] = send(after(blocks[6], have[4]), 6)
        join = lambda *group: jnp.concatenate([have[index] for index in group], axis=0)
        early = join(0, 4, 5, 1)
        best = score([early], [((0,), [0], False)])
        have[7] = send(after(blocks[7], best), 7)
        first_other, second_other = swap(join(0, 4)), swap(join(1, 5))
        mid = join(2, 3, 6)
        near_other = swap(join(2, 3))
        best = score([early, mid], [((0,), [1], True), ((1,), [0, 1], False)], best)
        best = score([early, mid, first_other, near_other], [((0, 1), [2, 3], True)], best)
        late = have[7] = after(have[7], best)
        late_other = swap(join(6, 7))
        best = score(
            [early, mid, late, first_other, near_other, second_other],
            [((0, 1), [5], True), ((2,), [0, 1, 3, 4, 5], False)],
            best,
        )
        best = score(
            [early, mid, late, late_other], [((0, 1, 2), [2, 3], True)], best, [0, 4, 5, 1, 2, 3, 6, 7]
        )
        slots = packed[0]
    else:
        (outgoing,), (slots, _, _) = pack(cluster_of, embeddings, [(0, clusters)], clusters, capacity, mixed)
        own = lax.all_to_all(
            outgoing.reshape(clusters, capacity, -1), "owners", 0, 0, axis_index_groups=same_core, tiled=True
        ).reshape(SLOTS, -1)
        other = by_xor(own, "owners", 1)
        best = score([own], [((0,), [0], False)])
        best = score([own, other], [((0,), [1], True)], best).reshape(clusters, capacity)
    answers = lax.all_to_all(best, "owners", 0, 0, axis_index_groups=same_core, tiled=True)
    return lookup(slots, answers, capacity, mixed)


def solution(mesh):
    placed = (P(("groups", "owners"), None), P(("groups", "owners")))
    return jax.shard_map(
        on_device, mesh=mesh, in_specs=placed, out_specs=P(("groups", "owners")), check_vma=False
    )
```

```python
import functools

import jax
import jax.numpy as jnp
from jax import lax
from jax.experimental import pallas as pl
from jax.experimental.pallas import tpu as pltpu
from jax.sharding import PartitionSpec as P

SLOTS = 1024
FLOOR = -4.0
DEAD = 4.0
VMEM_LIMIT = 40 * 2**20
LANES = 128


def row_slots(relative, clusters, capacity):
    rows = relative.shape[1]
    ids = lax.broadcasted_iota(jnp.int32, (clusters, LANES), 0)
    earlier = (
        lax.broadcasted_iota(jnp.int32, (LANES, LANES), 0)
        < lax.broadcasted_iota(jnp.int32, (LANES, LANES), 1)
    ).astype(jnp.bfloat16)
    carry = jnp.zeros((clusters, 1), jnp.float32)
    places = []
    for first in range(0, rows, LANES):
        part = relative[:, first : first + LANES]
        member = (ids == part).astype(jnp.float32)
        before = carry + jnp.dot(
            member.astype(jnp.bfloat16), earlier, preferred_element_type=jnp.float32
        )
        place = jnp.sum(before * member, axis=0, keepdims=True)
        places.append(part * capacity + place.astype(jnp.int32))
        carry = carry + jnp.sum(member, axis=1, keepdims=True)
    return jnp.concatenate(places, axis=1), carry


def picks(slots, taken, capacity, pick_ref):
    done = 0
    for first, count in taken:
        size = count * capacity
        wanted = lax.broadcasted_iota(jnp.int32, (size, slots.shape[1]), 0) + first * capacity
        pick_ref[done : done + size, :] = (wanted == slots).astype(jnp.float32).astype(jnp.bfloat16)
        done += size


def select(taken, capacity, counts, pick_ref, unit_ref, block_refs):
    lane = lax.broadcasted_iota(jnp.int32, (capacity, LANES), 1)
    place = lax.broadcasted_iota(jnp.int32, (capacity, LANES), 0).astype(jnp.float32)
    done = 0
    for block_ref, (first, count) in zip(block_refs, taken):
        for index in range(count):
            block = jnp.dot(
                pick_ref[done : done + capacity, :], unit_ref[...], preferred_element_type=jnp.float32
            )
            full = counts[first + index : first + index + 1, :]
            mark = jnp.where((place >= full) & (lane == 0), DEAD, 0.0)
            start = index * capacity
            block_ref[start : start + capacity, :LANES] = (block[:, :LANES] + mark).astype(jnp.bfloat16)
            block_ref[start : start + capacity, LANES:] = block[:, LANES:].astype(jnp.bfloat16)
            done += capacity


def pack_kernel(taken, mixed, clusters, capacity, cluster_ref, rows_ref, *refs):
    *block_refs, slot_ref, count_ref, unit_ref, ids_ref, held_ref, pick_ref, sems = refs
    steps, tile, _ = held_ref.shape
    ids_copy = pltpu.make_async_copy(cluster_ref, ids_ref, sems.at[steps])
    ids_copy.start()
    copies = [
        pltpu.make_async_copy(rows_ref.at[pl.ds(step * tile, tile), :], held_ref.at[step], sems.at[step])
        for step in range(steps)
    ]
    for copy in copies:
        copy.start()
    ids_copy.wait()
    relative = ids_ref[...].reshape(1, steps * tile)
    if mixed:
        relative = lax.bitwise_xor(relative, lax.axis_index("owners") // 2)
    slots, counts = row_slots(relative, clusters, capacity)
    slot_ref[...] = slots
    count_ref[...] = jnp.broadcast_to(counts, count_ref.shape)
    picks(slots, taken, capacity, pick_ref)
    for step, copy in enumerate(copies):
        copy.wait()
        values = held_ref[step]
        scale = lax.rsqrt(jnp.sum(values * values, axis=1, keepdims=True) + 1e-06)
        unit_ref[step * tile : (step + 1) * tile, :] = (values * scale).astype(jnp.bfloat16)
    select(taken, capacity, counts, pick_ref, unit_ref, block_refs)


def pack_cost(taken, capacity, rows, width):
    total = sum(count for _, count in taken) * capacity
    return pl.CostEstimate(
        flops=2 * total * rows * width, bytes_accessed=rows * width * 4 + total * width * 2, transcendentals=rows
    )


def block_shapes(taken, capacity, width):
    return [jax.ShapeDtypeStruct((count * capacity, width), jnp.bfloat16) for _, count in taken]


def pack(cluster_of, embeddings, taken, clusters, capacity, mixed):
    rows, width = embeddings.shape
    steps = 3 if rows % 384 == 0 else 1
    total = sum(count for _, count in taken) * capacity
    vmem = pl.BlockSpec(memory_space=pltpu.VMEM)
    *blocks, slots, counts, unit = pl.pallas_call(
        functools.partial(pack_kernel, taken, mixed, clusters, capacity),
        in_specs=[pl.BlockSpec(memory_space=pl.ANY)] * 2,
        out_specs=[vmem] * (len(taken) + 3),
        out_shape=block_shapes(taken, capacity, width)
        + [
            jax.ShapeDtypeStruct((1, rows), jnp.int32),
            jax.ShapeDtypeStruct((clusters, LANES), jnp.float32),
            jax.ShapeDtypeStruct((rows, width), jnp.bfloat16),
        ],
        scratch_shapes=[
            pltpu.VMEM((rows,), jnp.int32),
            pltpu.VMEM((steps, rows // steps, width), jnp.float32),
            pltpu.VMEM((total, rows), jnp.bfloat16),
            pltpu.SemaphoreType.DMA((steps + 1,)),
        ],
        compiler_params=pltpu.CompilerParams(vmem_limit_bytes=VMEM_LIMIT),
        cost_estimate=pack_cost(taken, capacity, rows, width),
    )(
        pltpu.with_memory_space_constraint(cluster_of, pltpu.HBM),
        pltpu.with_memory_space_constraint(embeddings, pltpu.HBM),
    )
    return blocks, (slots, counts, unit)


def more_kernel(taken, capacity, slot_ref, count_ref, unit_ref, *refs):
    *block_refs, pick_ref = refs
    picks(slot_ref[...], taken, capacity, pick_ref)
    select(taken, capacity, count_ref[...], pick_ref, unit_ref, block_refs)


def pack_more(packed, taken, capacity):
    rows, width = packed[2].shape
    total = sum(count for _, count in taken) * capacity
    vmem = pl.BlockSpec(memory_space=pltpu.VMEM)
    return pl.pallas_call(
        functools.partial(more_kernel, taken, capacity),
        in_specs=[vmem] * 3,
        out_specs=[vmem] * len(taken),
        out_shape=block_shapes(taken, capacity, width),
        scratch_shapes=[pltpu.VMEM((total, rows), jnp.bfloat16)],
        compiler_params=pltpu.CompilerParams(vmem_limit_bytes=VMEM_LIMIT),
        cost_estimate=pack_cost(taken, capacity, rows, width),
    )(*packed)


def pieces(refs, tile):
    groups, current, held = [], [], 0
    for ref in refs:
        start = 0
        while start < ref.shape[0]:
            size = min(tile - held, ref.shape[0] - start)
            current.append((ref, start, size))
            start += size
            held += size
            if held == tile:
                groups.append(current)
                current, held = [], 0
    if current:
        groups.append(current)
    return groups


def load(group):
    parts = [ref[start : start + size, :] for ref, start, size in group]
    return parts[0] if len(parts) == 1 else jnp.concatenate(parts, axis=0)


def own_rows(shape, key_group, query_group):
    found = None
    key_at = 0
    for key_ref, key_start, key_size in key_group:
        query_at = 0
        for query_ref, query_start, query_size in query_group:
            if key_ref is query_ref and key_start < query_start + query_size and query_start < key_start + key_size:
                row = lax.broadcasted_iota(jnp.int32, shape, 0)
                lane = lax.broadcasted_iota(jnp.int32, shape, 1)
                same = row - lane == query_start - query_at - key_start + key_at
                if key_size < shape[0]:
                    same = same & (row >= key_at) & (row < key_at + key_size)
                if query_size < shape[1]:
                    same = same & (lane >= query_at) & (lane < query_at + query_size)
                found = same if found is None else found | same
            query_at += query_size
        key_at += key_size
    return found


def tile_best(key_group, query_group, query):
    key = load(key_group)
    deep, wide = key.shape[0], query.shape[0]
    scores = lax.dot_general(key, query, (((1,), (1,)), ((), ())), preferred_element_type=jnp.float32)
    dead = key[:, :1].astype(jnp.float32) > 2.0
    scores = scores + jnp.where(dead, 2 * FLOOR, 0.0)
    own = own_rows(scores.shape, key_group, query_group)
    if own is not None:
        scores = jnp.where(own, FLOOR, scores)
    return jnp.max(scores.reshape(deep // 8, 8, wide), axis=0)


def score_kernel(plan, n_blocks, has_start, order, *refs):
    start_ref = refs[n_blocks] if has_start else None
    best_ref = refs[-1]
    chip = lax.axis_index("owners") // 2 if order else 0
    index = 0
    for query_blocks, key_blocks, starts in plan:
        for query_group in pieces([refs[block] for block in query_blocks], 256):
            query = load(query_group)
            best = jnp.full((8, query.shape[0]), FLOOR, jnp.float32)
            for key_group in pieces([refs[block] for block in key_blocks], 512):
                best = jnp.maximum(best, tile_best(key_group, query_group, query))
            row = jnp.max(best, axis=0, keepdims=True)
            for lane in range(0, query.shape[0], LANES):
                part = row[:, lane : lane + LANES]
                if starts:
                    part = jnp.maximum(part, start_ref[index : index + 1, :])
                best_ref[pl.ds(lax.bitwise_xor(order[index], chip) if order else index, 1), :] = part
                index += 1


def score(blocks, plan, start=None, order=None):
    n_query = sum(blocks[query].shape[0] for queries, _, _ in plan for query in queries)
    pairs = sum(
        blocks[query].shape[0] * blocks[key].shape[0] for queries, keys, _ in plan for query in queries for key in keys
    )
    width = blocks[0].shape[1]
    args = [*blocks] + ([] if start is None else [start])
    return pl.pallas_call(
        functools.partial(score_kernel, plan, len(blocks), start is not None, order),
        in_specs=[pl.BlockSpec(memory_space=pltpu.VMEM)] * len(args),
        out_specs=pl.BlockSpec(memory_space=pltpu.VMEM),
        out_shape=jax.ShapeDtypeStruct((n_query // LANES, LANES), jnp.float32),
        compiler_params=pltpu.CompilerParams(vmem_limit_bytes=VMEM_LIMIT),
        cost_estimate=pl.CostEstimate(
            flops=2 * pairs * width,
            bytes_accessed=sum(block.size for block in blocks) * 2,
            transcendentals=0,
        ),
    )(*args)


def lookup_kernel(capacity, mixed, slot_ref, answer_ref, out_ref):
    slots = slot_ref[...]
    clusters = answer_ref.shape[0]
    shift = capacity.bit_length() - 1
    place = lax.bitwise_and(slots, capacity - 1)
    which = lax.shift_right_logical(slots, shift)
    if mixed:
        which = lax.bitwise_xor(which, lax.axis_index("owners") // 2)
    rows = slots.shape[1]
    pick = (lax.broadcasted_iota(jnp.int32, (capacity, rows), 0) == place).astype(jnp.float32).astype(jnp.bfloat16)
    rest = answer_ref[...]
    total = jnp.zeros((clusters, rows), jnp.float32)
    for _ in range(3):
        part = rest.astype(jnp.bfloat16)
        rest = rest - part.astype(jnp.float32)
        total = total + jnp.dot(part, pick, preferred_element_type=jnp.float32)
    mine = lax.broadcasted_iota(jnp.int32, (clusters, rows), 0) == which
    found = jnp.sum(jnp.where(mine, total, 0.0), axis=0, keepdims=True)
    out_ref[...] = jnp.maximum(found, -1.0).reshape(out_ref.shape)


def lookup(slots, answers, capacity, mixed):
    return pl.pallas_call(
        functools.partial(lookup_kernel, capacity, mixed),
        in_specs=[pl.BlockSpec(memory_space=pltpu.VMEM)] * 2,
        out_specs=pl.BlockSpec(memory_space=pltpu.VMEM),
        out_shape=jax.ShapeDtypeStruct((slots.shape[1],), jnp.float32),
        compiler_params=pltpu.CompilerParams(vmem_limit_bytes=VMEM_LIMIT),
    )(slots, answers)


def by_xor(value, axis, mask):
    return lax.ppermute(value, axis, [(source, source ^ mask) for source in range(lax.axis_size(axis))])


def after(value, *before):
    return lax.optimization_barrier((value, *before))[0]


def on_device(embeddings, cluster_of):
    owners = lax.axis_size("owners")
    clusters = owners // 2
    capacity = SLOTS // clusters
    same_core = [list(range(core, owners, 2)) for core in range(2)]
    mixed = clusters == 8
    if mixed:
        send = lambda block, mask: by_xor(block, "owners", 2 * mask)
        swap = lambda block: by_xor(block, "owners", 1)
        first, then = (4, 5), (0, 1, 2, 3, 6, 7)
        blocks = {}
        got, packed = pack(cluster_of, embeddings, [(index, 1) for index in first], clusters, capacity, mixed)
        blocks.update(zip(first, got))
        blocks.update(zip(then, pack_more(packed, [(index, 1) for index in then], capacity)))
        have = {0: blocks[0]}
        for index in (4, 5, 1, 2, 3):
            have[index] = send(blocks[index], index)
        have[6] = send(after(blocks[6], have[4]), 6)
        join = lambda *group: jnp.concatenate([have[index] for index in group], axis=0)
        early = join(0, 4, 5, 1)
        best = score([early], [((0,), [0], False)])
        have[7] = send(after(blocks[7], best), 7)
        first_other, second_other = swap(join(0, 4)), swap(join(1, 5))
        mid = join(2, 3, 6)
        near_other = swap(join(2, 3))
        best = score([early, mid], [((0,), [1], True), ((1,), [0, 1], False)], best)
        best = score([early, mid, first_other, near_other], [((0, 1), [2, 3], True)], best)
        late = have[7] = after(have[7], best)
        six_other, late_other = swap(have[6]), swap(late)
        best = score(
            [early, mid, late, first_other, near_other, second_other, six_other],
            [((0, 1), [5, 6], True), ((2,), [0, 1, 3, 4, 5, 6], False)],
            best,
        )
        best = score(
            [early, mid, late, late_other], [((0, 1, 2), [2, 3], True)], best, [0, 4, 5, 1, 2, 3, 6, 7]
        )
        slots = packed[0]
    else:
        (outgoing,), (slots, _, _) = pack(cluster_of, embeddings, [(0, clusters)], clusters, capacity, mixed)
        own = lax.all_to_all(
            outgoing.reshape(clusters, capacity, -1), "owners", 0, 0, axis_index_groups=same_core, tiled=True
        ).reshape(SLOTS, -1)
        other = by_xor(own, "owners", 1)
        best = score([own], [((0,), [0], False)])
        best = score([own, other], [((0,), [1], True)], best).reshape(clusters, capacity)
    answers = lax.all_to_all(best, "owners", 0, 0, axis_index_groups=same_core, tiled=True)
    return lookup(slots, answers, capacity, mixed)


def solution(mesh):
    placed = (P(("groups", "owners"), None), P(("groups", "owners")))
    return jax.shard_map(
        on_device, mesh=mesh, in_specs=placed, out_specs=P(("groups", "owners")), check_vma=False
    )
```
